32 devices in a mesh: groups: 2 (over y), cache: 4 (over z), heads: 2 (over x), pair: 2 (over core).
Axes of the slice: x: 2, y: 2, z: 4, core: 2. Of those that a mesh axis runs over, the one named last changes fastest.
Arguments:
- queries: bfloat16 [3328, 8192], P(('groups', 'cache'), ('heads', 'pair')), parts along dimension 0, may hold values from -6 to 6
- new_keys: bfloat16 [3328, 1024], P(('groups', 'cache'), ('heads', 'pair')), parts along dimension 0, may hold values from -6 to 6
- new_values: bfloat16 [3328, 1024], P(('groups', 'cache'), ('heads', 'pair')), parts along dimension 0, may hold values from -6 to 6
- cache_keys: bfloat16 [64, 256, 1024], P(('groups', 'cache', 'pair'), None, 'heads'), parts along dimension 0, may hold values from -6 to 6
- cache_values: bfloat16 [64, 256, 1024], P(('groups', 'cache', 'pair'), None, 'heads'), parts along dimension 0, may hold values from -6 to 6
- request_pass: int32 [16, 8], P(('groups', 'cache')), parts along dimension 0, may hold values from 0 to 31, as said below
- rec_block: int32 [16, 1], P(('groups', 'cache')), parts along dimension 0, may hold values from 0 to 15, as said below
- passage_slot: int32 [64], P('groups'), parts along dimension 0, may hold values from 0 to 31, as said below
Outputs:
- attention: bfloat16 [3328, 8192], P(('groups', 'cache'), ('heads', 'pair')), parts along dimension 0
The draws below stay inside these ranges and needn't reach their ends.
There are 2 independent parts, one for each index of `groups`. The reference program is written for one: setup_inputs(seed, part) draws one part's arguments, and reference() takes and returns one part's arrays. A program takes and returns all parts, laid end to end along the dimension named above; each array names one. Nothing has to cross between parts.
Inputs may be any that keep to these rules, and one draw needn't show every extreme that they name: `request_pass`: the 16 passages named by the requests of one index of cache are distinct. An owner of slot s is the device s // 4 of cache and pair together; of those passages every owner holds 2 or 1, and some owner exactly 2. `passage_slot`: A permutation. `rec_block`: within each request distinct and increasing.
All inputs are finite; a program needn't handle non-finite values.
Results may differ from the reference program's by a relative error of at most 0.0038.
Values may be sent and summed in bfloat16 or wider, within the bound.
A program may use at most 64 MiB of HBM per device.

```python
import math
import jax
import jax.numpy as jnp
from jax import lax

HD = 128
QH = 64
KVH = 8
BLOCK = 128
TOPP = 8
PLEN = 256
RECB = 1
QLEN = 80
REQ_DEV = 2
OWNERS = 8
CAP = 2
PASS_DEV = 4
PASSAGES = 32
REQS = 8
CTX = 2048
NKEYS = 2128
ROWS_REQ = 208
QROWS = 1664


def routing(key):
    key_slot, key_owner, key_local = jax.random.split(jax.random.fold_in(key, 101), 3)
    slot_of = jax.random.permutation(key_slot, PASSAGES).astype(jnp.int32)
    passage_at = jnp.argsort(slot_of).astype(jnp.int32)
    cache_rows = REQS // REQ_DEV
    ref_total = REQ_DEV * TOPP
    orders = jax.vmap(lambda one_key: jax.random.permutation(one_key, OWNERS))(jax.random.split(key_owner, cache_rows))
    counter = jnp.arange(ref_total)
    owner_ids = orders[:, counter % OWNERS]
    rank_in = counter // OWNERS
    samples = jax.random.randint(key_local, (3, cache_rows, ref_total), 0, PASS_DEV // CAP)
    local_ids = jnp.min(samples, axis=0) * CAP + rank_in[None, :]
    slot_ids = owner_ids * PASS_DEV + local_ids
    pass_lists = passage_at[slot_ids].reshape(REQS, TOPP)
    return (slot_of, pass_lists.astype(jnp.int32))


def draw_request_pass(key, part):
    return routing(key)[1]


def draw_passage_slot(key, part):
    return routing(key)[0]


def draw_rec_block(key, part):
    key = jax.random.fold_in(key, 7)
    block_total = TOPP * PLEN // BLOCK
    orders = jax.vmap(lambda one_key: jax.random.permutation(one_key, block_total))(jax.random.split(key, REQS))
    orders = orders[:, :RECB].astype(jnp.int32)
    upper_rest = jax.random.permutation(jax.random.fold_in(key, 11), block_total - 1)[:RECB - 1].astype(jnp.int32)
    upper_row = jnp.concatenate((upper_rest, jnp.full((1,), block_total - 1, jnp.int32)))
    lower_rest = (jax.random.permutation(jax.random.fold_in(key, 13), block_total - 1)[:RECB - 1] + 1).astype(jnp.int32)
    lower_row = jnp.concatenate((jnp.zeros((1,), jnp.int32), lower_rest))
    orders = orders.at[0].set(upper_row).at[1].set(lower_row)
    return jnp.sort(orders, axis=1).astype(jnp.int32)


def draw_queries(key, part):
    key = jax.random.fold_in(key, 3)
    return jnp.clip(jax.random.normal(key, (QROWS, QH * HD), jnp.float32), -6.0, 6.0).astype(jnp.bfloat16)


def draw_cache_keys(key, part):
    key = jax.random.fold_in(key, 5)
    return jnp.clip(jax.random.normal(key, (PASSAGES, PLEN, KVH * HD), jnp.float32), -6.0, 6.0).astype(jnp.bfloat16)


def level_of(own_key, dims, cuts, least, top_value):
    gain = 1.0
    for dim, blocks in cuts:
        draws = jax.random.uniform(jax.random.fold_in(jax.random.fold_in(own_key, 6), dim), (blocks,), jnp.float32, least / len(cuts), top_value / len(cuts))
        gain = gain * jnp.repeat(jnp.exp(draws), dims[dim] // blocks).reshape((-1,) + (1,) * (len(dims) - 1 - dim))
    return gain


def scatter_about(rng, shape, spread, reach, shards=(), kind=jnp.bfloat16):
    drawn = spread * jax.random.normal(rng, shape, jnp.float32)
    if shards:
        drawn = drawn * level_of(rng, shape, shards, -0.22, 0.18)
    return jnp.clip(drawn, -reach, reach).astype(kind)


def setup_inputs(seed: int = 0, part: int = 0) -> dict:
    splits = jax.random.split(jax.random.key(seed), 9)
    part_splits = jax.random.split(jax.random.fold_in(splits[8], part), 9)
    return {
        "queries": draw_queries(jax.random.fold_in(jax.random.fold_in(splits[8], part), 71), part),
        "new_keys": scatter_about(part_splits[1], (QROWS, KVH * HD), 1.0, 6.0, ((0, 4), (1, 4))),
        "new_values": scatter_about(part_splits[2], (QROWS, KVH * HD), 1.0, 6.0, ((0, 4), (1, 4))),
        "cache_keys": draw_cache_keys(jax.random.fold_in(jax.random.fold_in(splits[8], part), 71), part),
        "cache_values": scatter_about(part_splits[4], (PASSAGES, PLEN, KVH * HD), 1.0, 6.0, ((0, 8), (2, 2))),
        "request_pass": draw_request_pass(jax.random.fold_in(jax.random.fold_in(splits[8], part), 71), part),
        "rec_block": draw_rec_block(jax.random.fold_in(jax.random.fold_in(splits[8], part), 71), part),
        "passage_slot": draw_passage_slot(jax.random.fold_in(jax.random.fold_in(splits[8], part), 71), part),
    }


def reference(queries, new_keys, new_values, cache_keys, cache_values, request_pass, rec_block, passage_slot):
    group_size = QH // KVH
    key_scale = 1.0 / math.sqrt(HD)

    def one_request(inputs):
        request_queries, fresh_keys, fresh_values, passes, blocks = inputs
        slot_ids = jnp.take(passage_slot, passes)
        context_keys = jnp.take(cache_keys, slot_ids, axis=0).reshape(CTX, KVH * HD)
        context_values = jnp.take(cache_values, slot_ids, axis=0).reshape(CTX, KVH * HD)
        for replaced in range(RECB):
            start_row = (blocks[replaced] * BLOCK).astype(jnp.int32)
            context_keys = lax.dynamic_update_slice(context_keys, fresh_keys[replaced * BLOCK:(replaced + 1) * BLOCK], (start_row, jnp.int32(0)))
            context_values = lax.dynamic_update_slice(context_values, fresh_values[replaced * BLOCK:(replaced + 1) * BLOCK], (start_row, jnp.int32(0)))
        key_rows = jnp.concatenate((context_keys, fresh_keys[RECB * BLOCK:]), axis=0)
        value_rows = jnp.concatenate((context_values, fresh_values[RECB * BLOCK:]), axis=0)
        block_pos = (blocks[:, None] * BLOCK + jnp.arange(BLOCK, dtype=jnp.int32)[None, :]).reshape(-1)
        query_pos = jnp.concatenate((block_pos.astype(jnp.int32), CTX + jnp.arange(QLEN, dtype=jnp.int32)))
        query_wide = request_queries.astype(jnp.float32).reshape(ROWS_REQ, KVH, group_size, HD)
        key_wide = key_rows.astype(jnp.float32).reshape(NKEYS, KVH, HD)
        value_wide = value_rows.astype(jnp.float32).reshape(NKEYS, KVH, HD)
        scores = jnp.einsum('rgqd,kgd->gqrk', query_wide, key_wide) * key_scale
        visible = jnp.arange(NKEYS, dtype=jnp.int32)[None, :] <= query_pos[:, None]
        scores = jnp.where(visible[None, None], scores, -jnp.inf)
        row_max = lax.optimization_barrier(jnp.max(scores, axis=3, keepdims=True))
        weights = jnp.exp(scores - row_max)
        totals = lax.optimization_barrier(jnp.sum(weights, axis=3, keepdims=True))
        rounded = lax.optimization_barrier(weights.astype(jnp.bfloat16)).astype(jnp.float32)
        mixed_rows = jnp.einsum('gqrk,kgd->rgqd', rounded, value_wide) / jnp.transpose(totals, (2, 0, 1, 3))
        return mixed_rows.reshape(ROWS_REQ, QH * HD).astype(jnp.bfloat16)
    results = lax.map(one_request, (queries.reshape(REQS, ROWS_REQ, QH * HD), new_keys.reshape(REQS, ROWS_REQ, KVH * HD), new_values.reshape(REQS, ROWS_REQ, KVH * HD), request_pass, rec_block))
    return results.reshape(QROWS, QH * HD)
```

```python
import functools
import math

import jax
import jax.numpy as jnp
from jax import lax
from jax.experimental import pallas as pl
from jax.experimental.pallas import tpu as pltpu
from jax.sharding import PartitionSpec as P

HD = 128
BLOCK = 128
MESH = pl.DeviceIdType.MESH
F32 = jnp.float32


def flip(index, step, count):
    total = 0
    bit = 1
    while bit < count:
        total = total + bit * ((index // bit + step // bit) % 2)
        bit *= 2
    return total


def nt_dot(a, b):
    return lax.dot_general(a, b, (((1,), (1,)), ((), ())), preferred_element_type=F32)


def kernel(
    dims,
    q_hbm,
    nk_hbm,
    nv_hbm,
    ck_hbm,
    cv_hbm,
    rp_ref,
    rb_ref,
    ps_ref,
    out_ref,
    q_v,
    nk_v,
    nv_v,
    ck_v,
    cv_v,
    lists,
    jtab,
    send,
    kvbuf,
    qarr,
    m_ref,
    l_ref,
    acc_ref,
    in_sem,
    list_send,
    list_recv,
    send_sem,
    recv_sem,
):
    cache_n, pair_n, reqs, per_req, rooms, pass_dev, pass_len, kvw, rows = dims
    heads = kvw // HD
    group = q_hbm.shape[1] // kvw
    quest = rows - BLOCK
    rec_lanes = group * BLOCK
    lanes = group * rows
    refs = reqs * per_req
    gain = math.log2(math.e) / math.sqrt(HD)
    zc = lax.axis_index("cache")
    zp = lax.axis_index("pair")
    me = zc * pair_n + zp

    loads = [
        pltpu.make_async_copy(src, dst, in_sem.at[i])
        for i, (src, dst) in enumerate(
            ((ck_hbm, ck_v), (cv_hbm, cv_v), (q_hbm, q_v), (nk_hbm, nk_v), (nv_hbm, nv_v))
        )
    ]
    for load in loads:
        load.start()

    barrier = pltpu.get_barrier_semaphore()

    def greet(step, _):
        peer = flip(zc, step // pair_n, cache_n)
        core = (zp + step) % pair_n
        pl.semaphore_signal(
            barrier, inc=1, device_id={"cache": peer, "pair": core}, device_id_type=MESH
        )
        return 0

    lax.fori_loop(1, cache_n * pair_n, greet, 0)
    pl.semaphore_wait(barrier, cache_n * pair_n - 1)

    def list_copy(step, index):
        peer = flip(zc, step, cache_n)
        return pltpu.make_async_remote_copy(
            src_ref=rp_ref,
            dst_ref=lists.at[index],
            send_sem=list_send.at[step],
            recv_sem=list_recv.at[index],
            device_id={"cache": peer, "pair": zp},
            device_id_type=MESH,
        )

    def list_start(step, _):
        list_copy(step, zc).start()
        return 0

    lax.fori_loop(1, cache_n, list_start, 0)
    for load in loads[:2]:
        load.wait()

    def picks(slot_of):
        count = jnp.int32(0)
        chosen = [jnp.int32(0)] * rooms
        for j in range(refs):
            slot = slot_of(j)
            match = slot // pass_dev == me
            for r in range(rooms):
                chosen[r] = jnp.where(match & (count == r), slot % pass_dev, chosen[r])
            count = count + match.astype(jnp.int32)
        return chosen

    def data_copy(step, peer, core, r):
        return pltpu.make_async_remote_copy(
            src_ref=send.at[step, core, r],
            dst_ref=kvbuf.at[me, r],
            send_sem=send_sem.at[step, core, r],
            recv_sem=recv_sem.at[me, r],
            device_id={"cache": peer, "pair": core},
            device_id_type=MESH,
        )

    def fill(dst, pick, core):
        span = pl.ds(pl.multiple_of(core * kvw, kvw), kvw)
        dst[0] = ck_v[pick, :, span]
        dst[1] = cv_v[pick, :, span]

    own = picks(lambda j: ps_ref[rp_ref[j // per_req, j % per_req]])

    def send_step(step):
        peer = flip(zc, step, cache_n)
        list_copy(step, peer).wait_recv()
        chosen = picks(lambda j: ps_ref[lists[peer, j // per_req, j % per_req]])
        for r in range(rooms):
            for core in range(pair_n):
                fill(send.at[step, core, r], chosen[r], core)
                data_copy(step, peer, core, r).start()

    if cache_n == 4:
        for step in (2, 3, 1):
            send_step(step)
    else:
        lax.fori_loop(1, cache_n, lambda step, _: (send_step(step), 0)[1], 0)

    for r in range(rooms):
        for away in range(1, pair_n):
            core = (zp + away) % pair_n
            fill(send.at[0, core, r], own[r], core)
            data_copy(0, zc, core, r).start()
        fill(kvbuf.at[me, r], own[r], zp)

    def seek(owner, _):
        count = jnp.int32(0)
        found = [jnp.int32(-1)] * rooms
        for j in range(refs):
            match = ps_ref[rp_ref[j // per_req, j % per_req]] // pass_dev == owner
            for r in range(rooms):
                found[r] = jnp.where(match & (count == r), j, found[r])
            count = count + match.astype(jnp.int32)
        for r in range(rooms):
            jtab[owner * rooms + r] = found[r]
        return 0

    lax.fori_loop(0, cache_n * pair_n, seek, 0)

    for load in loads[2:]:
        load.wait()
    for i in range(reqs):
        for g in range(heads):
            for h in range(group):
                col = pl.ds((g * group + h) * HD, HD)
                qarr[i, g, pl.ds(h * BLOCK, BLOCK)] = q_v[pl.ds(i * rows, BLOCK), col]
                qarr[i, g, pl.ds(rec_lanes + h * quest, quest)] = q_v[
                    pl.ds(i * rows + BLOCK, quest), col
                ]

    tiles = []
    for start, stop in ((0, rec_lanes), (rec_lanes, lanes)):
        at = start
        while at < stop:
            width = min(256, stop - at)
            tiles.append((at, width))
            at += width

    for i in range(reqs):
        for g in range(heads):
            col = pl.ds(g * HD, HD)
            for at, width in tiles:
                depth = BLOCK if at < rec_lanes else rows
                keys = nk_v[pl.ds(i * rows, depth), col]
                values = nv_v[pl.ds(i * rows, depth), col]
                scores = nt_dot(keys, qarr[i, g, pl.ds(at, width)])
                key_row = lax.broadcasted_iota(jnp.int32, (depth, width), 0)
                lane = lax.broadcasted_iota(jnp.int32, (depth, width), 1)
                if at < rec_lanes:
                    own_row = (lane + at) % BLOCK
                else:
                    own_row = (lane + (at - rec_lanes)) % quest + BLOCK
                scores = jnp.where(key_row <= own_row, scores, -jnp.inf)
                top = jnp.max(scores, axis=0, keepdims=True)
                weights = jnp.exp2(scores * gain - top * gain)
                m_ref[i, g, :, pl.ds(at, width)] = top
                l_ref[i, g, :, pl.ds(at, width)] = jnp.sum(weights, axis=0, keepdims=True)
                acc_ref[i, g, :, pl.ds(at, width)] = jnp.dot(
                    values.T, weights.astype(jnp.bfloat16), preferred_element_type=F32
                )

    def chunk(owner, r):
        j = jtab[owner * rooms + r]
        valid = j >= 0
        j = jnp.maximum(j, 0)
        req = j // per_req
        blocks = pass_len // BLOCK
        first = (j % per_req) * blocks
        fresh = rb_ref[req, 0]
        shown = [
            (valid & (first + b < fresh), valid & (first + b != fresh)) for b in range(blocks)
        ]
        for g in range(heads):
            col = pl.ds(g * HD, HD)
            keys = kvbuf[owner, r, 0, :, col]
            values_t = kvbuf[owner, r, 1, :, col].T
            for at, width in tiles:
                kind = 0 if at < rec_lanes else 1
                span = pl.ds(at, width)
                scores = nt_dot(keys, qarr[req, g, span])
                old_top = m_ref[req, g, :, span]
                top = old_top
                for b in range(blocks):
                    part = jnp.max(scores[b * BLOCK : (b + 1) * BLOCK], axis=0, keepdims=True)
                    top = jnp.maximum(top, jnp.where(shown[b][kind], part, -jnp.inf))
                scaled = top * gain
                pieces = []
                total = jnp.zeros_like(top)
                for b in range(blocks):
                    shift = jnp.where(shown[b][kind], scaled, jnp.inf)
                    piece = jnp.exp2(scores[b * BLOCK : (b + 1) * BLOCK] * gain - shift)
                    total = total + jnp.sum(piece, axis=0, keepdims=True)
                    pieces.append(piece.astype(jnp.bfloat16))
                weights = jnp.concatenate(pieces, axis=0)
                decay = jnp.exp2(old_top * gain - scaled)
                total = l_ref[req, g, :, span] * decay + total
                mixed = jnp.dot(values_t, weights, preferred_element_type=F32)
                mixed = acc_ref[req, g, :, span] * decay + mixed
                for i in range(reqs):
                    mine = req == i
                    m_ref[i, g, :, span] = jnp.where(mine, top, m_ref[i, g, :, span])
                    l_ref[i, g, :, span] = jnp.where(mine, total, l_ref[i, g, :, span])
                    acc_ref[i, g, :, span] = jnp.where(mine, mixed, acc_ref[i, g, :, span])

    for r in range(rooms):
        chunk(me, r)

    def arrive(step, core, r):
        owner = flip(zc, step, cache_n) * pair_n + core
        pltpu.make_async_remote_copy(
            src_ref=send.at[0, 0, r],
            dst_ref=kvbuf.at[owner, r],
            send_sem=send_sem.at[0, 0, r],
            recv_sem=recv_sem.at[owner, r],
            device_id={"cache": owner // pair_n, "pair": core},
            device_id_type=MESH,
        ).wait_recv()
        chunk(owner, r)

    for away in range(1, pair_n):
        for r in range(rooms):
            arrive(0, (zp + away) % pair_n, r)

    def take(t, _):
        step = t // (rooms * pair_n)
        if cache_n == 4:
            step = 2 + step - 3 * (step // 2)
        else:
            step = step + 1
        arrive(step, t % pair_n, t // pair_n % rooms)
        return 0

    lax.fori_loop(0, (cache_n - 1) * rooms * pair_n, take, 0)

    for i in range(reqs):
        for g in range(heads):
            for h in range(group):
                span = pl.ds(h * BLOCK, BLOCK)
                done = acc_ref[i, g, :, span] / l_ref[i, g, :, span]
                out_ref[pl.ds(i * rows, BLOCK), pl.ds((g * group + h) * HD, HD)] = done.T.astype(
                    out_ref.dtype
                )
            span = pl.ds(rec_lanes, lanes - rec_lanes)
            done = (acc_ref[i, g, :, span] / l_ref[i, g, :, span]).T.astype(out_ref.dtype)
            for h in range(group):
                out_ref[pl.ds(i * rows + BLOCK, quest), pl.ds((g * group + h) * HD, HD)] = done[
                    h * quest : (h + 1) * quest
                ]

    def list_end(step, _):
        list_copy(step, zc).wait_send()
        return 0

    lax.fori_loop(1, cache_n, list_end, 0)

    def data_end(step, _):
        for core in range(pair_n):
            for r in range(rooms):
                data_copy(step, zc, core, r).wait_send()
        return 0

    lax.fori_loop(1, cache_n, data_end, 0)
    for away in range(1, pair_n):
        for r in range(rooms):
            data_copy(0, zc, (zp + away) % pair_n, r).wait_send()


def on_device(
    queries, new_keys, new_values, cache_keys, cache_values, request_pass, rec_block, passage_slot
):
    reqs, per_req = request_pass.shape
    cache_n = lax.axis_size("cache")
    pair_n = lax.axis_size("pair")
    owners = cache_n * pair_n
    rooms = max(1, (reqs * per_req + owners - 1) // owners)
    pass_dev, pass_len, cache_width = cache_keys.shape
    kvw = cache_width // pair_n
    rows = queries.shape[0] // reqs
    heads = kvw // HD
    lanes = queries.shape[1] // kvw * rows
    dims = (cache_n, pair_n, reqs, per_req, rooms, pass_dev, pass_len, kvw, rows)
    bf16 = jnp.bfloat16
    hbm = pl.BlockSpec(memory_space=pl.ANY)
    smem = pl.BlockSpec(memory_space=pltpu.SMEM)
    return pl.pallas_call(
        functools.partial(kernel, dims),
        out_shape=jax.ShapeDtypeStruct(queries.shape, bf16),
        in_specs=[hbm] * 5 + [smem] * 3,
        out_specs=pl.BlockSpec(memory_space=pltpu.VMEM),
        scratch_shapes=[
            pltpu.VMEM(queries.shape, bf16),
            pltpu.VMEM(new_keys.shape, bf16),
            pltpu.VMEM(new_values.shape, bf16),
            pltpu.VMEM(cache_keys.shape, bf16),
            pltpu.VMEM(cache_values.shape, bf16),
            pltpu.SMEM((cache_n, reqs, per_req), jnp.int32),
            pltpu.SMEM((owners * rooms,), jnp.int32),
            pltpu.VMEM((cache_n, pair_n, rooms, 2, pass_len, kvw), bf16),
            pltpu.VMEM((owners, rooms, 2, pass_len, kvw), bf16),
            pltpu.VMEM((reqs, heads, lanes, HD), bf16),
            pltpu.VMEM((reqs, heads, 1, lanes), F32),
            pltpu.VMEM((reqs, heads, 1, lanes), F32),
            pltpu.VMEM((reqs, heads, HD, lanes), F32),
            pltpu.SemaphoreType.DMA((5,)),
            pltpu.SemaphoreType.DMA((cache_n,)),
            pltpu.SemaphoreType.DMA((cache_n,)),
            pltpu.SemaphoreType.DMA((cache_n, pair_n, rooms)),
            pltpu.SemaphoreType.DMA((owners, rooms)),
        ],
        compiler_params=pltpu.CompilerParams(
            collective_id=0, has_side_effects=True, vmem_limit_bytes=48 * 1024 * 1024
        ),
    )(
        queries,
        new_keys,
        new_values,
        cache_keys,
        cache_values,
        request_pass,
        rec_block,
        passage_slot,
    )


def solution(mesh):
    return jax.shard_map(
        on_device,
        mesh=mesh,
        in_specs=(
            P(("groups", "cache"), ("heads", "pair")),
            P(("groups", "cache"), ("heads", "pair")),
            P(("groups", "cache"), ("heads", "pair")),
            P(("groups", "cache", "pair"), None, "heads"),
            P(("groups", "cache", "pair"), None, "heads"),
            P(("groups", "cache"), None),
            P(("groups", "cache"), None),
            P("groups"),
        ),
        out_specs=P(("groups", "cache"), ("heads", "pair")),
        check_vma=False,
    )
```

```python
import functools
import math

import jax
import jax.numpy as jnp
from jax import lax
from jax.experimental import pallas as pl
from jax.experimental.pallas import tpu as pltpu
from jax.sharding import PartitionSpec as P

HD = 128
BLOCK = 128
MESH = pl.DeviceIdType.MESH
F32 = jnp.float32


def flip(index, step, count):
    total = 0
    bit = 1
    while bit < count:
        total = total + bit * ((index // bit + step // bit) % 2)
        bit *= 2
    return total


def nt_dot(a, b):
    return lax.dot_general(a, b, (((1,), (1,)), ((), ())), preferred_element_type=F32)


def kernel(
    dims,
    q_hbm,
    nk_hbm,
    nv_hbm,
    ck_hbm,
    cv_hbm,
    rp_ref,
    rb_ref,
    ps_ref,
    out_ref,
    q_v,
    nk_v,
    nv_v,
    ck_v,
    cv_v,
    lists,
    jtab,
    send,
    kvbuf,
    qarr,
    m_ref,
    l_ref,
    acc_ref,
    in_sem,
    list_send,
    list_recv,
    send_sem,
    recv_sem,
):
    cache_n, pair_n, reqs, per_req, rooms, pass_dev, pass_len, kvw, rows = dims
    heads = kvw // HD
    group = q_hbm.shape[1] // kvw
    quest = rows - BLOCK
    rec_lanes = group * BLOCK
    lanes = group * rows
    refs = reqs * per_req
    gain = math.log2(math.e) / math.sqrt(HD)
    zc = lax.axis_index("cache")
    zp = lax.axis_index("pair")
    me = zc * pair_n + zp

    loads = [
        pltpu.make_async_copy(src, dst, in_sem.at[i])
        for i, (src, dst) in enumerate(
            ((ck_hbm, ck_v), (cv_hbm, cv_v), (q_hbm, q_v), (nk_hbm, nk_v), (nv_hbm, nv_v))
        )
    ]
    for load in loads:
        load.start()

    barrier = pltpu.get_barrier_semaphore()

    def greet(step, _):
        peer = flip(zc, step // pair_n, cache_n)
        core = (zp + step) % pair_n
        pl.semaphore_signal(
            barrier, inc=1, device_id={"cache": peer, "pair": core}, device_id_type=MESH
        )
        return 0

    lax.fori_loop(1, cache_n * pair_n, greet, 0)
    pl.semaphore_wait(barrier, cache_n * pair_n - 1)

    def list_copy(step, index):
        peer = flip(zc, step, cache_n)
        return pltpu.make_async_remote_copy(
            src_ref=rp_ref,
            dst_ref=lists.at[index],
            send_sem=list_send.at[step],
            recv_sem=list_recv.at[index],
            device_id={"cache": peer, "pair": zp},
            device_id_type=MESH,
        )

    def list_start(step, _):
        list_copy(step, zc).start()
        return 0

    lax.fori_loop(1, cache_n, list_start, 0)
    for load in loads[:2]:
        load.wait()

    def picks(slot_of):
        count = jnp.int32(0)
        chosen = [jnp.int32(0)] * rooms
        for j in range(refs):
            slot = slot_of(j)
            match = slot // pass_dev == me
            for r in range(rooms):
                chosen[r] = jnp.where(match & (count == r), slot % pass_dev, chosen[r])
            count = count + match.astype(jnp.int32)
        return chosen

    def data_copy(step, peer, core, r):
        return pltpu.make_async_remote_copy(
            src_ref=send.at[step, core, r],
            dst_ref=kvbuf.at[me, r],
            send_sem=send_sem.at[step, core, r],
            recv_sem=recv_sem.at[me, r],
            device_id={"cache": peer, "pair": core},
            device_id_type=MESH,
        )

    def fill(dst, pick, core):
        span = pl.ds(pl.multiple_of(core * kvw, kvw), kvw)
        dst[0] = ck_v[pick, :, span]
        dst[1] = cv_v[pick, :, span]

    own = picks(lambda j: ps_ref[rp_ref[j // per_req, j % per_req]])

    def send_step(step):
        peer = flip(zc, step, cache_n)
        list_copy(step, peer).wait_recv()
        chosen = picks(lambda j: ps_ref[lists[peer, j // per_req, j % per_req]])
        for r in range(rooms):
            for core in range(pair_n):
                fill(send.at[step, core, r], chosen[r], core)
                data_copy(step, peer, core, r).start()

    if cache_n == 4:
        for step in (2, 3, 1):
            send_step(step)
    else:
        lax.fori_loop(1, cache_n, lambda step, _: (send_step(step), 0)[1], 0)

    for r in range(rooms):
        for away in range(1, pair_n):
            core = (zp + away) % pair_n
            fill(send.at[0, core, r], own[r], core)
            data_copy(0, zc, core, r).start()
        fill(kvbuf.at[me, r], own[r], zp)

    def seek(owner, _):
        count = jnp.int32(0)
        found = [jnp.int32(-1)] * rooms
        for j in range(refs):
            match = ps_ref[rp_ref[j // per_req, j % per_req]] // pass_dev == owner
            for r in range(rooms):
                found[r] = jnp.where(match & (count == r), j, found[r])
            count = count + match.astype(jnp.int32)
        for r in range(rooms):
            jtab[owner * rooms + r] = found[r]
        return 0

    lax.fori_loop(0, cache_n * pair_n, seek, 0)

    for load in loads[2:]:
        load.wait()
    for i in range(reqs):
        for g in range(heads):
            for h in range(group):
                col = pl.ds((g * group + h) * HD, HD)
                qarr[i, g, pl.ds(h * BLOCK, BLOCK)] = q_v[pl.ds(i * rows, BLOCK), col]
                qarr[i, g, pl.ds(rec_lanes + h * quest, quest)] = q_v[
                    pl.ds(i * rows + BLOCK, quest), col
                ]

    tiles = []
    for start, stop in ((0, rec_lanes), (rec_lanes, lanes)):
        at = start
        while at < stop:
            width = min(256, stop - at)
            tiles.append((at, width))
            at += width

    for i in range(reqs):
        for g in range(heads):
            col = pl.ds(g * HD, HD)
            for at, width in tiles:
                depth = BLOCK if at < rec_lanes else rows
                keys = nk_v[pl.ds(i * rows, depth), col]
                values = nv_v[pl.ds(i * rows, depth), col]
                scores = nt_dot(qarr[i, g, pl.ds(at, width)], keys)
                key_row = lax.broadcasted_iota(jnp.int32, (width, depth), 1)
                lane = lax.broadcasted_iota(jnp.int32, (width, depth), 0)
                if at < rec_lanes:
                    own_row = (lane + at) % BLOCK
                else:
                    own_row = (lane + (at - rec_lanes)) % quest + BLOCK
                scores = jnp.where(key_row <= own_row, scores, -jnp.inf)
                top = jnp.max(scores, axis=1, keepdims=True)
                weights = jnp.exp2(scores * gain - top * gain)
                total = jnp.sum(weights, axis=1, keepdims=True) * (1.0 / HD)
                m_ref[i, g, pl.ds(at, width)] = jnp.broadcast_to(top, (width, HD))
                l_ref[i, g, pl.ds(at, width)] = jnp.broadcast_to(total, (width, HD))
                acc_ref[i, g, pl.ds(at, width)] = jnp.dot(
                    weights.astype(jnp.bfloat16), values, preferred_element_type=F32
                )

    def chunk(owner, r):
        j = jtab[owner * rooms + r]
        valid = j >= 0
        j = jnp.maximum(j, 0)
        req = j // per_req
        blocks = pass_len // BLOCK
        first = (j % per_req) * blocks
        fresh = rb_ref[req, 0]
        shown = [
            (valid & (first + b < fresh), valid & (first + b != fresh)) for b in range(blocks)
        ]
        for g in range(heads):
            col = pl.ds(g * HD, HD)
            keys = kvbuf[owner, r, 0, :, col]
            values = kvbuf[owner, r, 1, :, col]
            for at, width in tiles:
                kind = 0 if at < rec_lanes else 1
                span = pl.ds(at, width)
                scores = nt_dot(qarr[req, g, span], keys)
                parts = [scores[:, b * BLOCK : (b + 1) * BLOCK] for b in range(blocks)]
                best = jnp.where(shown[0][kind], parts[0], -jnp.inf)
                for b in range(1, blocks):
                    best = jnp.maximum(best, jnp.where(shown[b][kind], parts[b], -jnp.inf))
                old_top = m_ref[req, g, span]
                top = jnp.maximum(old_top, jnp.max(best, axis=1, keepdims=True))
                scaled = top * gain
                pieces = []
                decay = jnp.exp2(old_top * gain - scaled)
                total = l_ref[req, g, span] * decay
                for b in range(blocks):
                    shift = jnp.where(shown[b][kind], scaled, jnp.inf)
                    piece = jnp.exp2(parts[b] * gain - shift)
                    total = total + piece
                    pieces.append(piece.astype(jnp.bfloat16))
                weights = jnp.concatenate(pieces, axis=1)
                mixed = jnp.dot(weights, values, preferred_element_type=F32)
                mixed = acc_ref[req, g, span] * decay + mixed
                for i in range(reqs):
                    mine = req == i
                    m_ref[i, g, span] = jnp.where(mine, top, m_ref[i, g, span])
                    l_ref[i, g, span] = jnp.where(mine, total, l_ref[i, g, span])
                    acc_ref[i, g, span] = jnp.where(mine, mixed, acc_ref[i, g, span])

    for r in range(rooms):
        chunk(me, r)

    def arrive(step, core, r):
        owner = flip(zc, step, cache_n) * pair_n + core
        pltpu.make_async_remote_copy(
            src_ref=send.at[0, 0, r],
            dst_ref=kvbuf.at[owner, r],
            send_sem=send_sem.at[0, 0, r],
            recv_sem=recv_sem.at[owner, r],
            device_id={"cache": owner // pair_n, "pair": core},
            device_id_type=MESH,
        ).wait_recv()
        chunk(owner, r)

    for away in range(1, pair_n):
        for r in range(rooms):
            arrive(0, (zp + away) % pair_n, r)

    def take(t, _):
        step = t // (rooms * pair_n)
        if cache_n == 4:
            step = 2 + step - 3 * (step // 2)
        else:
            step = step + 1
        arrive(step, t % pair_n, t // pair_n % rooms)
        return 0

    lax.fori_loop(0, (cache_n - 1) * rooms * pair_n, take, 0)

    for i in range(reqs):
        for g in range(heads):
            for h in range(group):
                col = pl.ds((g * group + h) * HD, HD)
                for at, to, size in (
                    (h * BLOCK, i * rows, BLOCK),
                    (rec_lanes + h * quest, i * rows + BLOCK, quest),
                ):
                    span = pl.ds(at, size)
                    total = jnp.sum(l_ref[i, g, span], axis=1, keepdims=True)
                    out_ref[pl.ds(to, size), col] = (acc_ref[i, g, span] / total).astype(
                        out_ref.dtype
                    )

    def list_end(step, _):
        list_copy(step, zc).wait_send()
        return 0

    lax.fori_loop(1, cache_n, list_end, 0)

    def data_end(step, _):
        for core in range(pair_n):
            for r in range(rooms):
                data_copy(step, zc, core, r).wait_send()
        return 0

    lax.fori_loop(1, cache_n, data_end, 0)
    for away in range(1, pair_n):
        for r in range(rooms):
            data_copy(0, zc, (zp + away) % pair_n, r).wait_send()


def on_device(
    queries, new_keys, new_values, cache_keys, cache_values, request_pass, rec_block, passage_slot
):
    reqs, per_req = request_pass.shape
    cache_n = lax.axis_size("cache")
    pair_n = lax.axis_size("pair")
    owners = cache_n * pair_n
    rooms = max(1, (reqs * per_req + owners - 1) // owners)
    pass_dev, pass_len, cache_width = cache_keys.shape
    kvw = cache_width // pair_n
    rows = queries.shape[0] // reqs
    heads = kvw // HD
    lanes = queries.shape[1] // kvw * rows
    dims = (cache_n, pair_n, reqs, per_req, rooms, pass_dev, pass_len, kvw, rows)
    bf16 = jnp.bfloat16
    hbm = pl.BlockSpec(memory_space=pl.ANY)
    smem = pl.BlockSpec(memory_space=pltpu.SMEM)
    return pl.pallas_call(
        functools.partial(kernel, dims),
        out_shape=jax.ShapeDtypeStruct(queries.shape, bf16),
        in_specs=[hbm] * 5 + [smem] * 3,
        out_specs=pl.BlockSpec(memory_space=pltpu.VMEM),
        scratch_shapes=[
            pltpu.VMEM(queries.shape, bf16),
            pltpu.VMEM(new_keys.shape, bf16),
            pltpu.VMEM(new_values.shape, bf16),
            pltpu.VMEM(cache_keys.shape, bf16),
            pltpu.VMEM(cache_values.shape, bf16),
            pltpu.SMEM((cache_n, reqs, per_req), jnp.int32),
            pltpu.SMEM((owners * rooms,), jnp.int32),
            pltpu.VMEM((cache_n, pair_n, rooms, 2, pass_len, kvw), bf16),
            pltpu.VMEM((owners, rooms, 2, pass_len, kvw), bf16),
            pltpu.VMEM((reqs, heads, lanes, HD), bf16),
            pltpu.VMEM((reqs, heads, lanes, HD), F32),
            pltpu.VMEM((reqs, heads, lanes, HD), F32),
            pltpu.VMEM((reqs, heads, lanes, HD), F32),
            pltpu.SemaphoreType.DMA((5,)),
            pltpu.SemaphoreType.DMA((cache_n,)),
            pltpu.SemaphoreType.DMA((cache_n,)),
            pltpu.SemaphoreType.DMA((cache_n, pair_n, rooms)),
            pltpu.SemaphoreType.DMA((owners, rooms)),
        ],
        compiler_params=pltpu.CompilerParams(
            collective_id=0, has_side_effects=True, vmem_limit_bytes=48 * 1024 * 1024
        ),
    )(
        queries,
        new_keys,
        new_values,
        cache_keys,
        cache_values,
        request_pass,
        rec_block,
        passage_slot,
    )


def solution(mesh):
    return jax.shard_map(
        on_device,
        mesh=mesh,
        in_specs=(
            P(("groups", "cache"), ("heads", "pair")),
            P(("groups", "cache"), ("heads", "pair")),
            P(("groups", "cache"), ("heads", "pair")),
            P(("groups", "cache", "pair"), None, "heads"),
            P(("groups", "cache", "pair"), None, "heads"),
            P(("groups", "cache"), None),
            P(("groups", "cache"), None),
            P("groups"),
        ),
        out_specs=P(("groups", "cache"), ("heads", "pair")),
        check_vma=False,
    )
```

```python
import functools
import math

import jax
import jax.numpy as jnp
from jax import lax
from jax.experimental import pallas as pl
from jax.experimental.pallas import tpu as pltpu
from jax.sharding import PartitionSpec as P

HD = 128
BLOCK = 128
MESH = pl.DeviceIdType.MESH
F32 = jnp.float32


def flip(index, step, count):
    total = 0
    bit = 1
    while bit < count:
        total = total + bit * ((index // bit + step // bit) % 2)
        bit *= 2
    return total


def nt_dot(a, b):
    return lax.dot_general(a, b, (((1,), (1,)), ((), ())), preferred_element_type=F32)


def kernel(
    dims,
    q_hbm,
    nk_hbm,
    nv_hbm,
    ck_hbm,
    cv_hbm,
    rp_ref,
    rb_ref,
    ps_ref,
    out_ref,
    q_v,
    nk_v,
    nv_v,
    ck_v,
    cv_v,
    lists,
    jtab,
    send,
    kvbuf,
    qarr,
    m_ref,
    l_ref,
    acc_ref,
    in_sem,
    list_send,
    list_recv,
    send_sem,
    recv_sem,
):
    cache_n, pair_n, reqs, per_req, rooms, pass_dev, pass_len, kvw, rows = dims
    heads = kvw // HD
    group = q_hbm.shape[1] // kvw
    quest = rows - BLOCK
    rec_lanes = group * BLOCK
    lanes = group * rows
    refs = reqs * per_req
    gain = math.log2(math.e) / math.sqrt(HD)
    zc = lax.axis_index("cache")
    zp = lax.axis_index("pair")
    me = zc * pair_n + zp

    loads = [
        pltpu.make_async_copy(src, dst, in_sem.at[i])
        for i, (src, dst) in enumerate(
            ((ck_hbm, ck_v), (cv_hbm, cv_v), (q_hbm, q_v), (nk_hbm, nk_v), (nv_hbm, nv_v))
        )
    ]
    for load in loads:
        load.start()

    barrier = pltpu.get_barrier_semaphore()

    def greet(step, _):
        peer = flip(zc, step // pair_n, cache_n)
        core = (zp + step) % pair_n
        pl.semaphore_signal(
            barrier, inc=1, device_id={"cache": peer, "pair": core}, device_id_type=MESH
        )
        return 0

    lax.fori_loop(1, cache_n * pair_n, greet, 0)
    pl.semaphore_wait(barrier, cache_n * pair_n - 1)

    def list_copy(step, index):
        peer = flip(zc, step, cache_n)
        return pltpu.make_async_remote_copy(
            src_ref=rp_ref,
            dst_ref=lists.at[index],
            send_sem=list_send.at[step],
            recv_sem=list_recv.at[index],
            device_id={"cache": peer, "pair": zp},
            device_id_type=MESH,
        )

    def list_start(step, _):
        list_copy(step, zc).start()
        return 0

    lax.fori_loop(1, cache_n, list_start, 0)
    for load in loads[:2]:
        load.wait()

    def picks(slot_of):
        count = jnp.int32(0)
        chosen = [jnp.int32(0)] * rooms
        for j in range(refs):
            slot = slot_of(j)
            match = slot // pass_dev == me
            for r in range(rooms):
                chosen[r] = jnp.where(match & (count == r), slot % pass_dev, chosen[r])
            count = count + match.astype(jnp.int32)
        return chosen

    def data_copy(step, peer, core, r):
        return pltpu.make_async_remote_copy(
            src_ref=send.at[step, core, r],
            dst_ref=kvbuf.at[me, r],
            send_sem=send_sem.at[step, core, r],
            recv_sem=recv_sem.at[me, r],
            device_id={"cache": peer, "pair": core},
            device_id_type=MESH,
        )

    def fill(dst, pick, core):
        span = pl.ds(pl.multiple_of(core * kvw, kvw), kvw)
        dst[0] = ck_v[pick, :, span]
        dst[1] = cv_v[pick, :, span]

    own = picks(lambda j: ps_ref[rp_ref[j // per_req, j % per_req]])

    def send_step(step):
        peer = flip(zc, step, cache_n)
        list_copy(step, peer).wait_recv()
        chosen = picks(lambda j: ps_ref[lists[peer, j // per_req, j % per_req]])
        for r in range(rooms):
            for core in range(pair_n):
                fill(send.at[step, core, r], chosen[r], core)
                data_copy(step, peer, core, r).start()

    if cache_n == 4:
        for turn in range(3):
            send_step((turn + 1 - zp) % 3 + 1)
    else:
        lax.fori_loop(1, cache_n, lambda step, _: (send_step(step), 0)[1], 0)

    for r in range(rooms):
        for away in range(1, pair_n):
            core = (zp + away) % pair_n
            fill(send.at[0, core, r], own[r], core)
            data_copy(0, zc, core, r).start()
        fill(kvbuf.at[me, r], own[r], zp)

    def seek(owner, _):
        count = jnp.int32(0)
        found = [jnp.int32(-1)] * rooms
        for j in range(refs):
            match = ps_ref[rp_ref[j // per_req, j % per_req]] // pass_dev == owner
            for r in range(rooms):
                found[r] = jnp.where(match & (count == r), j, found[r])
            count = count + match.astype(jnp.int32)
        for r in range(rooms):
            jtab[owner * rooms + r] = found[r]
        return 0

    lax.fori_loop(0, cache_n * pair_n, seek, 0)

    for load in loads[2:]:
        load.wait()
    for i in range(reqs):
        for g in range(heads):
            for h in range(group):
                col = pl.ds((g * group + h) * HD, HD)
                qarr[i, g, pl.ds(h * BLOCK, BLOCK)] = q_v[pl.ds(i * rows, BLOCK), col]
                qarr[i, g, pl.ds(rec_lanes + h * quest, quest)] = q_v[
                    pl.ds(i * rows + BLOCK, quest), col
                ]

    tiles = []
    for start, stop in ((0, rec_lanes), (rec_lanes, lanes)):
        at = start
        while at < stop:
            width = min(256, stop - at)
            tiles.append((at, width))
            at += width

    for i in range(reqs):
        for g in range(heads):
            col = pl.ds(g * HD, HD)
            for at, width in tiles:
                depth = BLOCK if at < rec_lanes else rows
                keys = nk_v[pl.ds(i * rows, depth), col]
                values = nv_v[pl.ds(i * rows, depth), col]
                scores = nt_dot(qarr[i, g, pl.ds(at, width)], keys)
                key_row = lax.broadcasted_iota(jnp.int32, (width, depth), 1)
                lane = lax.broadcasted_iota(jnp.int32, (width, depth), 0)
                if at < rec_lanes:
                    own_row = (lane + at) % BLOCK
                else:
                    own_row = (lane + (at - rec_lanes)) % quest + BLOCK
                scores = jnp.where(key_row <= own_row, scores, -jnp.inf)
                top = jnp.max(scores, axis=1, keepdims=True)
                weights = jnp.exp2(scores * gain - top * gain)
                total = jnp.sum(weights, axis=1, keepdims=True) * (1.0 / HD)
                m_ref[i, g, pl.ds(at, width)] = jnp.broadcast_to(top, (width, HD))
                l_ref[i, g, pl.ds(at, width)] = jnp.broadcast_to(total, (width, HD))
                acc_ref[i, g, pl.ds(at, width)] = jnp.dot(
                    weights.astype(jnp.bfloat16), values, preferred_element_type=F32
                )

    def chunk(owner, r):
        j = jtab[owner * rooms + r]
        valid = j >= 0
        j = jnp.maximum(j, 0)
        req = j // per_req
        blocks = pass_len // BLOCK
        first = (j % per_req) * blocks
        fresh = rb_ref[req, 0]
        shown = [
            (valid & (first + b < fresh), valid & (first + b != fresh)) for b in range(blocks)
        ]
        for g in range(heads):
            col = pl.ds(g * HD, HD)
            keys = kvbuf[owner, r, 0, :, col]
            values = kvbuf[owner, r, 1, :, col]
            for at, width in tiles:
                kind = 0 if at < rec_lanes else 1
                span = pl.ds(at, width)
                scores = nt_dot(qarr[req, g, span], keys)
                parts = [scores[:, b * BLOCK : (b + 1) * BLOCK] for b in range(blocks)]
                best = jnp.where(shown[0][kind], parts[0], -jnp.inf)
                for b in range(1, blocks):
                    best = jnp.maximum(best, jnp.where(shown[b][kind], parts[b], -jnp.inf))
                old_top = m_ref[req, g, span]
                top = jnp.maximum(old_top, jnp.max(best, axis=1, keepdims=True))
                scaled = top * gain
                pieces = []
                decay = jnp.exp2(old_top * gain - scaled)
                total = l_ref[req, g, span] * decay
                for b in range(blocks):
                    shift = jnp.where(shown[b][kind], scaled, jnp.inf)
                    piece = jnp.exp2(parts[b] * gain - shift)
                    total = total + piece
                    pieces.append(piece.astype(jnp.bfloat16))
                weights = jnp.concatenate(pieces, axis=1)
                mixed = jnp.dot(weights, values, preferred_element_type=F32)
                mixed = acc_ref[req, g, span] * decay + mixed
                for i in range(reqs):
                    mine = req == i
                    m_ref[i, g, span] = jnp.where(mine, top, m_ref[i, g, span])
                    l_ref[i, g, span] = jnp.where(mine, total, l_ref[i, g, span])
                    acc_ref[i, g, span] = jnp.where(mine, mixed, acc_ref[i, g, span])

    for r in range(rooms):
        chunk(me, r)

    def arrive(step, core, r):
        owner = flip(zc, step, cache_n) * pair_n + core
        pltpu.make_async_remote_copy(
            src_ref=send.at[0, 0, r],
            dst_ref=kvbuf.at[owner, r],
            send_sem=send_sem.at[0, 0, r],
            recv_sem=recv_sem.at[owner, r],
            device_id={"cache": owner // pair_n, "pair": core},
            device_id_type=MESH,
        ).wait_recv()
        chunk(owner, r)

    for away in range(1, pair_n):
        for r in range(rooms):
            arrive(0, (zp + away) % pair_n, r)

    def take(t, _):
        step = t // (rooms * pair_n)
        if cache_n == 4:
            step = (step + 1 - t % pair_n) % 3 + 1
        else:
            step = step + 1
        arrive(step, t % pair_n, t // pair_n % rooms)
        return 0

    lax.fori_loop(0, (cache_n - 1) * rooms * pair_n, take, 0)

    for i in range(reqs):
        for g in range(heads):
            for h in range(group):
                col = pl.ds((g * group + h) * HD, HD)
                for at, to, size in (
                    (h * BLOCK, i * rows, BLOCK),
                    (rec_lanes + h * quest, i * rows + BLOCK, quest),
                ):
                    span = pl.ds(at, size)
                    total = jnp.sum(l_ref[i, g, span], axis=1, keepdims=True)
                    out_ref[pl.ds(to, size), col] = (acc_ref[i, g, span] / total).astype(
                        out_ref.dtype
                    )

    def list_end(step, _):
        list_copy(step, zc).wait_send()
        return 0

    lax.fori_loop(1, cache_n, list_end, 0)

    def data_end(step, _):
        for core in range(pair_n):
            for r in range(rooms):
                data_copy(step, zc, core, r).wait_send()
        return 0

    lax.fori_loop(1, cache_n, data_end, 0)
    for away in range(1, pair_n):
        for r in range(rooms):
            data_copy(0, zc, (zp + away) % pair_n, r).wait_send()


def on_device(
    queries, new_keys, new_values, cache_keys, cache_values, request_pass, rec_block, passage_slot
):
    reqs, per_req = request_pass.shape
    cache_n = lax.axis_size("cache")
    pair_n = lax.axis_size("pair")
    owners = cache_n * pair_n
    rooms = max(1, (reqs * per_req + owners - 1) // owners)
    pass_dev, pass_len, cache_width = cache_keys.shape
    kvw = cache_width // pair_n
    rows = queries.shape[0] // reqs
    heads = kvw // HD
    lanes = queries.shape[1] // kvw * rows
    dims = (cache_n, pair_n, reqs, per_req, rooms, pass_dev, pass_len, kvw, rows)
    bf16 = jnp.bfloat16
    hbm = pl.BlockSpec(memory_space=pl.ANY)
    smem = pl.BlockSpec(memory_space=pltpu.SMEM)
    return pl.pallas_call(
        functools.partial(kernel, dims),
        out_shape=jax.ShapeDtypeStruct(queries.shape, bf16),
        in_specs=[hbm] * 5 + [smem] * 3,
        out_specs=pl.BlockSpec(memory_space=pltpu.VMEM),
        scratch_shapes=[
            pltpu.VMEM(queries.shape, bf16),
            pltpu.VMEM(new_keys.shape, bf16),
            pltpu.VMEM(new_values.shape, bf16),
            pltpu.VMEM(cache_keys.shape, bf16),
            pltpu.VMEM(cache_values.shape, bf16),
            pltpu.SMEM((cache_n, reqs, per_req), jnp.int32),
            pltpu.SMEM((owners * rooms,), jnp.int32),
            pltpu.VMEM((cache_n, pair_n, rooms, 2, pass_len, kvw), bf16),
            pltpu.VMEM((owners, rooms, 2, pass_len, kvw), bf16),
            pltpu.VMEM((reqs, heads, lanes, HD), bf16),
            pltpu.VMEM((reqs, heads, lanes, HD), F32),
            pltpu.VMEM((reqs, heads, lanes, HD), F32),
            pltpu.VMEM((reqs, heads, lanes, HD), F32),
            pltpu.SemaphoreType.DMA((5,)),
            pltpu.SemaphoreType.DMA((cache_n,)),
            pltpu.SemaphoreType.DMA((cache_n,)),
            pltpu.SemaphoreType.DMA((cache_n, pair_n, rooms)),
            pltpu.SemaphoreType.DMA((owners, rooms)),
        ],
        compiler_params=pltpu.CompilerParams(
            collective_id=0, has_side_effects=True, vmem_limit_bytes=48 * 1024 * 1024
        ),
    )(
        queries,
        new_keys,
        new_values,
        cache_keys,
        cache_values,
        request_pass,
        rec_block,
        passage_slot,
    )


def solution(mesh):
    return jax.shard_map(
        on_device,
        mesh=mesh,
        in_specs=(
            P(("groups", "cache"), ("heads", "pair")),
            P(("groups", "cache"), ("heads", "pair")),
            P(("groups", "cache"), ("heads", "pair")),
            P(("groups", "cache", "pair"), None, "heads"),
            P(("groups", "cache", "pair"), None, "heads"),
            P(("groups", "cache"), None),
            P(("groups", "cache"), None),
            P("groups"),
        ),
        out_specs=P(("groups", "cache"), ("heads", "pair")),
        check_vma=False,
    )
```
